32 devices in a mesh: groups: 2 (over y), space: 4 (over z), tm: 2 (over x), obs: 2 (over core).
Axes of the slice: x: 2, y: 2, z: 4, core: 2. Of those that a mesh axis runs over, the one named last changes fastest.
Arguments:
- footprint: bfloat16 [4, 4, 4, 256, 256], P('space', ('tm', 'obs')), may hold values from -0.1875 to 0.1875
- tile_index: int32 [8, 4, 4], P(('groups', 'space'), ('tm', 'obs')), parts along dimension 0, may hold values from 0 to 1
- assign: int32 [8, 4], P(('groups', 'tm', 'obs')), parts along dimension 0, may hold values from 0 to 3, each once within a row
- land: int32 [4], P('space'), may hold values 0 or 1
- sigma: float32 [16, 128], P(('groups', 'space')), parts along dimension 0, may hold values from 0.3 to 1.5
- departures: float32 [8, 4, 256, 128], P(('groups', 'tm', 'obs'), 'space'), parts along dimension 0, may hold values from -6 to 6
- rinv: float32 [8, 4, 256], P(('groups', 'tm', 'obs'), 'space'), parts along dimension 0, may hold values from 0.25 to 2
- alpha: float32 [4, 128], P('groups'), parts along dimension 0, may hold values from 0.1 to 0.4
- beta: float32 [2, 128], P('groups'), parts along dimension 0, may hold values from 0.2 to 0.8
Outputs:
- increment: float32 [8, 8, 128, 128], P(('groups', 'tm'), 'space'), parts along dimension 0
- weighted: float32 [8, 4, 256, 128], P(('groups', 'tm', 'obs'), 'space'), parts along dimension 0
The draws below stay inside these ranges and needn't reach their ends.
There are 2 independent parts, one for each index of `groups`. The reference program is written for one: setup_inputs(seed, part) draws one part's arguments, and reference() takes and returns one part's arrays. A program takes and returns all parts, laid end to end along the dimension named above; an argument that names none is the same for every part. Nothing has to cross between parts.
Inputs may be any that keep to these rules, and one draw needn't show every extreme that they name: `assign`: each row holds every block number once.
All inputs are finite; a program needn't handle non-finite values. No bound on the sum of `land` on one device may be relied on, other than what follows from the above.
Results may differ from the reference program's by a relative error of at most 0.017.
Values may be sent and summed in bfloat16 or wider, within the bound.
A program may use at most 64 MiB of HBM per device.

```python
import math
import jax
import jax.numpy as jnp
from jax import lax

TILE = 256
COLS = 128
M = 128
TW = 2
RD = 2
ITERS = 2
TIMES = 4
ROWS = 8
TILE_ROWS = 4
FT = 2
OBC = 4
WC = 4
SPACE_DEV = 4
N_SPACE = 4
N_TM = 2
N_OBS = 2


def set_ends(values, key, smallest, largest):
    dims = values.shape
    place = [jax.random.randint(jax.random.fold_in(key, axis), (), 0, dims[axis]) for axis in range(len(dims))]
    values = values.at[tuple(place)].set(smallest)
    longest = dims.index(max(dims))
    place[longest] = (place[longest] + 1) % dims[longest]
    return values.at[tuple(place)].set(largest)


def shard_levels(stream_key, shape, cuts, smallest, high):
    loudness, own = 1.0, jax.random.fold_in(stream_key, 6)
    for position, parts in cuts:
        steps = jnp.exp(jax.random.uniform(jax.random.fold_in(own, position), (parts,), jnp.float32, smallest / len(cuts), high / len(cuts)))
        loudness = loudness * jnp.repeat(steps, shape[position] // parts).reshape([-1 if axis == position else 1 for axis in range(len(shape))])
    return loudness


def noise(own_key, dims, scale, bound, cuts=(), kind=jnp.bfloat16):
    factor_of = shard_levels(own_key, dims, cuts, -0.22, 0.18) if cuts else 1.0
    drawn = jax.random.normal(own_key, dims, jnp.float32) * scale * factor_of
    return jnp.minimum(jnp.maximum(drawn, -bound), bound).astype(kind)


def setup_inputs(seed: int = 0, part: int = 0) -> dict:
    keys = jax.random.split(jax.random.key(seed), 10)
    part_keys = jax.random.split(jax.random.fold_in(keys[9], part), 10)
    return {
        "footprint": noise(keys[0], (SPACE_DEV, WC, OBC, TILE, TILE), (TILE * SPACE_DEV) ** -0.5, 0.1875, ((0, 4), (1, 4))),
        "tile_index": set_ends(jax.random.randint(part_keys[1], (SPACE_DEV, WC, OBC), 0, FT), jax.random.fold_in(part_keys[1], 1), 0, FT - 1).astype(jnp.int32),
        "assign": jax.vmap(lambda own: jax.random.permutation(own, OBC))(jax.random.split(part_keys[2], WC)).reshape((WC, OBC)).astype(jnp.int32),
        "land": set_ends((jax.random.randint(keys[3], (TILE_ROWS,), 0, 2) < 1).astype(jnp.int32), jax.random.fold_in(keys[3], 1), 0, 1),
        "sigma": jnp.clip(jnp.exp(math.log(1.5) - 1.60943787 * jax.random.uniform(part_keys[4], (ROWS, COLS), jnp.float32) ** shard_levels(part_keys[4], (ROWS, COLS), ((0, 4),), -0.2, 0.2)), 0.3, 1.5),
        "departures": noise(part_keys[5], (WC, OBC, TILE, M), 1.0, 6.0, ((0, 4), (1, 4)), jnp.float32),
        "rinv": jnp.clip(jnp.exp(math.log(2.0) - 2.0794415 * jax.random.uniform(part_keys[6], (WC, OBC, TILE), jnp.float32) ** shard_levels(part_keys[6], (WC, OBC, TILE), ((0, 4), (1, 4)), -0.2, 0.2)), 0.25, 2.0),
        "alpha": jnp.clip(jnp.exp(jax.random.uniform(part_keys[7], (ITERS, M), jnp.float32, math.log(0.1), math.log(0.4))), 0.1, 0.4),
        "beta": jnp.clip(jax.random.uniform(part_keys[8], (ITERS - 1, M), jnp.float32, 0.2, 0.8), 0.2, 0.8),
    }


OCEAN = 0.35
SPATIAL = 0.2
TEMPORAL = 0.6


def smooth_grid(field):
    padded = jnp.pad(field, ((0, 0), (1, 1), (1, 1), (0, 0)))
    beside_all = padded[:, 2:, 1:-1] + padded[:, :-2, 1:-1] + padded[:, 1:-1, 2:] + padded[:, 1:-1, :-2]
    return field + SPATIAL * beside_all


def to_tiles(field):
    split = field.reshape(N_TM, TW, N_SPACE, RD, COLS, M)
    split = jnp.transpose(split, (2, 0, 1, 3, 4, 5))
    return split.reshape(N_SPACE, N_TM, FT, TILE, M)


def from_tiles(tiles):
    split = tiles.reshape(N_SPACE, N_TM, TW, RD, COLS, M)
    split = jnp.transpose(split, (1, 2, 0, 3, 4, 5))
    return split.reshape(TIMES, ROWS, COLS, M)


def reference(footprint, tile_index, assign, land, sigma, departures, rinv, alpha, beta):
    scale_rows = jnp.repeat(jnp.where(land == 1, 1.0, OCEAN).astype(jnp.float32), ROWS // TILE_ROWS)
    spread = (sigma * scale_rows[:, None])[None, :, :, None]
    weights = rinv[:, :, :, None]

    def correlate(field):
        before = jnp.concatenate([jnp.zeros_like(field[:1]), field[:-1]], axis=0)
        return spread * smooth_grid(field + TEMPORAL * before)

    def correlate_adjoint(field):
        smoothed = smooth_grid(spread * field)
        after = jnp.concatenate([smoothed[1:], jnp.zeros_like(smoothed[:1])], axis=0)
        return smoothed + TEMPORAL * after

    def forward(field):
        cells = to_tiles(field).astype(jnp.bfloat16)

        def one(carry, pieces):
            tiles_s, which_s, cells_s = pieces
            per_col = jnp.repeat(cells_s, N_OBS, axis=0)
            chosen = jnp.take_along_axis(per_col, which_s[:, :, None, None], axis=1)
            term = jnp.einsum("cbij,cbjm->cbim", tiles_s.astype(jnp.float32), chosen.astype(jnp.float32))
            rounded = lax.optimization_barrier(term.astype(jnp.bfloat16))
            return carry + rounded.astype(jnp.float32), None

        start = jnp.zeros((WC, OBC, TILE, M), jnp.float32)
        total, _ = lax.scan(one, start, (footprint, tile_index, cells))
        return jnp.take_along_axis(total, assign[:, :, None, None], axis=1)

    def adjoint(rounded):
        back = jnp.argsort(assign, axis=1)
        by_block = jnp.take_along_axis(rounded, back[:, :, None, None], axis=1).astype(jnp.float32)

        def one(pieces):
            tiles_s, which_s = pieces
            contrib = jnp.einsum("cbji,cbjm->cbim", tiles_s.astype(jnp.float32), by_block)
            picks = (which_s[:, None, :] == jnp.arange(FT)[None, :, None]).astype(jnp.float32)
            local = jnp.einsum("ctb,cbim->ctim", picks, contrib, precision=lax.Precision.HIGHEST)
            return jnp.sum(local.reshape(N_TM, N_OBS, FT, TILE, M), axis=1)

        grads = lax.map(one, (footprint, tile_index))
        return correlate_adjoint(from_tiles(grads))

    def hessian(direction):
        fitted = forward(correlate(direction))
        return direction + adjoint((weights * fitted).astype(jnp.bfloat16))

    gradient = adjoint((weights * departures).astype(jnp.bfloat16))
    state = jnp.zeros_like(gradient)
    residual = gradient
    direction = gradient
    for step in range(ITERS):
        image = hessian(direction)
        state = state + alpha[step] * direction
        if step + 1 < ITERS:
            residual = residual - alpha[step] * image
            direction = residual + beta[step] * direction
    increment = correlate(state)
    fitted = forward(increment)
    return increment, weights * (fitted - departures)
```

```python
import functools

import jax
import jax.numpy as jnp
from jax import lax
from jax.experimental import pallas as pl
from jax.experimental.pallas import tpu as pltpu
from jax.sharding import PartitionSpec as P

MESH = pl.DeviceIdType.MESH

TW = 2
RD = 2

OCEAN = 0.35
SPATIAL = 0.2
TEMPORAL = 0.6
BF = jnp.bfloat16
F32 = jnp.float32


def kernel(
    n, nt, fp, which, order, land, sigma, dep, rinv, alpha, beta, inc, wout,
    fpt, spread, weights, cells, zsend, zrecv, psend, precv, osend, orecv, hsend, hrows, htime,
    zs, zr, ps, pr, os_, or_, hs, hr,
):
    s = lax.axis_index("space")
    k = lax.axis_index("tm")
    c = lax.axis_index("obs")
    cols = sigma.shape[1]
    low, high = s > 0, s < n - 1
    prev, nxt = k > 0, k < nt - 1
    both = jnp.logical_and

    hrows[...] = jnp.zeros_like(hrows)
    htime[...] = jnp.zeros_like(htime)

    barrier = pltpu.get_barrier_semaphore()
    partners = [(None, {"space": lax.rem(s + d, n)}) for d in range(1, n)]
    partners.append((None, {"obs": 1 - c}))
    partners.append((prev, {"tm": k - 1}))
    partners.append((nxt, {"tm": k + 1}))
    for sc, ds in ((low, -1), (high, 1)):
        for kc, dk in ((prev, -1), (nxt, 1)):
            partners.append((both(sc, kc), {"space": s + ds, "tm": k + dk}))

    def run_if(cond, action):
        if cond is None:
            action()
        else:
            pl.when(cond)(action)

    expected = 0
    for cond, target in partners:
        run_if(cond, functools.partial(
            pl.semaphore_signal, barrier, inc=1, device_id=target, device_id_type=MESH))
        expected = expected + (1 if cond is None else cond.astype(jnp.int32))

    scale = jnp.where(land[0] == 1, 1.0, OCEAN).astype(F32)
    for r in range(RD):
        spread[r] = jnp.broadcast_to(sigma[r:r + 1, :], (cols, cols)).T * scale
    height = weights.shape[0]
    lanes = weights.shape[1]
    for i in range(0, height, lanes):
        weights[i:i + lanes] = jnp.broadcast_to(rinv[0, :, i:i + lanes], (lanes, lanes)).T
    zsend[0] = (weights[...] * dep[0, 0]).astype(BF)

    pl.semaphore_wait(barrier, expected)
    pending = []

    def send(src, dst, ssem, rsem, target, cond=None):
        copy = pltpu.make_async_remote_copy(
            src_ref=src, dst_ref=dst, send_sem=ssem, recv_sem=rsem,
            device_id=target, device_id_type=MESH)
        run_if(cond, copy.start)
        pending.append((cond, copy))
        return copy

    def hops():
        return sorted(range(1, n), key=lambda d: -min(d, n - d))

    def gather_start(i):
        return {d: send(zsend.at[i], zrecv.at[i, d], zs.at[i, d], zr.at[i, d],
                        {"space": lax.rem(s + d, n)}) for d in hops()}

    def contribution(z, position):
        block = order[0, position]
        tile = which[0, 0, block]
        wide = z.astype(F32)
        parts = [wide * jnp.where(tile == t, 1.0, 0.0).astype(F32) for t in range(TW)]
        return jnp.dot(fpt[block], jnp.concatenate(parts, axis=1).astype(BF),
                       preferred_element_type=F32)

    def adjoint(i, copies):
        total = contribution(zsend[i], s)
        for d in reversed(hops()):
            copies[d].wait_recv()
            total = total + contribution(zrecv[i, d], lax.rem(s + n - d, n))
        for t in range(TW):
            osend[i, t] = total[:, t * lanes:(t + 1) * lanes].astype(BF)
        copy = send(osend.at[i], orecv.at[i], os_.at[i], or_.at[i], {"obs": 1 - c})
        copy.wait_recv()
        out = []
        for t in range(TW):
            tile = osend[i, t].astype(F32) + orecv[i, t].astype(F32)
            out.append([tile[r * cols:(r + 1) * cols] * spread[r] for r in range(RD)])
        return smooth(2 * i, out, False)

    def smooth(h, q, forward):
        for t in range(TW):
            for r in range(RD):
                hsend[h, t, r] = q[t][r].astype(BF)
        edge = TW - 1 if forward else 0
        step = 1 if forward else -1
        there, here = (nxt, prev) if forward else (prev, nxt)
        sides = ((high, low, 1, RD - 1, 0), (low, high, -1, 0, 1))
        waits = []
        for j, (to, frm, ds, row, side) in enumerate(sides):
            waits.append((frm, send(
                hsend.at[h, :, row], hrows.at[h, side, pl.ds(0, TW)], hs.at[h, j], hr.at[h, j],
                {"space": s + ds}, to)))
        for j, (to, frm, ds, row, side) in enumerate(sides):
            waits.append((both(frm, here), send(
                hsend.at[h, edge, row], hrows.at[h, side, TW], hs.at[h, 2 + j], hr.at[h, 2 + j],
                {"space": s + ds, "tm": k + step}, both(to, there))))
        waits.append((here, send(
            hsend.at[h, edge], htime.at[h], hs.at[h, 4], hr.at[h, 4], {"tm": k + step}, there)))
        for cond, copy in waits:
            run_if(cond, copy.wait_recv)
        at = lax.broadcasted_iota(jnp.int32, (cols, lanes), 0)
        out = []
        for t in range(TW):
            other = t - 1 if forward else t + 1
            inside = 0 <= other < TW
            slot = other if inside else TW
            rows = [hrows[h, 0, t].astype(F32) + TEMPORAL * hrows[h, 0, slot].astype(F32)]
            for r in range(RD):
                beside = q[other][r] if inside else htime[h, r].astype(F32)
                rows.append(q[t][r] + TEMPORAL * beside)
            rows.append(hrows[h, 1, t].astype(F32) + TEMPORAL * hrows[h, 1, slot].astype(F32))
            done = []
            for r in range(RD):
                u = rows[r + 1]
                left = jnp.where(at == 0, 0.0, pltpu.roll(u, 1, 0))
                right = jnp.where(at == cols - 1, 0.0, pltpu.roll(u, cols - 1, 0))
                done.append(u + SPATIAL * (rows[r] + rows[r + 2] + left + right))
            out.append(done)
        return out

    def correlate(h, field):
        done = smooth(h, field, True)
        return [[done[t][r] * spread[r] for r in range(RD)] for t in range(TW)]

    def observe(i, field):
        for t in range(TW):
            for r in range(RD):
                cells[i, t, r * cols:(r + 1) * cols] = field[t][r].astype(BF)

        def term(position):
            block = order[0, position]
            return jnp.dot(fp[0, 0, block], cells[i, which[0, 0, block]],
                           preferred_element_type=F32).astype(BF)

        copies = {}
        for d in hops():
            position = lax.rem(s + d, n)
            psend[i, d] = term(position)
            copies[d] = send(psend.at[i, d], precv.at[i, d], ps.at[i, d], pr.at[i, d],
                             {"space": position})
        total = term(s).astype(F32)
        for d in reversed(hops()):
            copies[d].wait_recv()
            total = total + precv[i, d].astype(F32)
        return total

    copies = gather_start(0)
    for b in range(n):
        fpt[b] = fp[0, 0, b].T
    gradient = adjoint(0, copies)
    zsend[1] = (weights[...] * observe(0, correlate(1, gradient))).astype(BF)
    image = adjoint(1, gather_start(1))
    first, second, turn = alpha[0:1, :], alpha[1:2, :], beta[0:1, :]
    state = []
    for t in range(TW):
        rows = []
        for r in range(RD):
            g = gradient[t][r]
            residual = g - first * (g + image[t][r])
            rows.append(first * g + second * (residual + turn * g))
        state.append(rows)
    increment = correlate(3, state)
    for t in range(TW):
        for r in range(RD):
            inc[t, r] = increment[t][r]
    fitted = observe(1, increment)
    wout[0, 0] = weights[...] * (fitted - dep[0, 0])
    for cond, copy in pending:
        run_if(cond, copy.wait_send)


def solution(mesh):
    n, nt = mesh.shape["space"], mesh.shape["tm"]

    def shards(footprint, tile_index, assign, land, sigma, departures, rinv, alpha, beta):
        blocks, width = footprint.shape[2], footprint.shape[3]
        cols, members = sigma.shape[1], alpha.shape[1]
        assert blocks == n and width == RD * cols and sigma.shape[0] == RD
        vmem = pl.BlockSpec(memory_space=pltpu.VMEM)
        smem = pl.BlockSpec(memory_space=pltpu.SMEM)
        dma = pltpu.SemaphoreType.DMA
        return pl.pallas_call(
            functools.partial(kernel, n, nt),
            out_shape=(
                jax.ShapeDtypeStruct((TW, RD, cols, members), F32),
                jax.ShapeDtypeStruct((1, 1, width, members), F32),
            ),
            in_specs=[vmem, smem, smem, smem, vmem, vmem, vmem, vmem, vmem],
            out_specs=(vmem, vmem),
            scratch_shapes=[
                pltpu.VMEM((n, width, width), BF),
                pltpu.VMEM((RD, cols, members), F32),
                pltpu.VMEM((width, members), F32),
                pltpu.VMEM((2, TW, width, members), BF),
                pltpu.VMEM((2, width, members), BF),
                pltpu.VMEM((2, n, width, members), BF),
                pltpu.VMEM((2, n, width, members), BF),
                pltpu.VMEM((2, n, width, members), BF),
                pltpu.VMEM((2, TW, width, members), BF),
                pltpu.VMEM((2, TW, width, members), BF),
                pltpu.VMEM((4, TW, RD, cols, members), BF),
                pltpu.VMEM((4, 2, TW + 1, cols, members), BF),
                pltpu.VMEM((4, RD, cols, members), BF),
                dma((2, n)), dma((2, n)), dma((2, n)), dma((2, n)),
                dma((2,)), dma((2,)), dma((4, 5)), dma((4, 5)),
            ],
            compiler_params=pltpu.CompilerParams(
                collective_id=0, has_side_effects=True, vmem_limit_bytes=40 * 1024 * 1024
            ),
        )(footprint, tile_index, assign, land, sigma, departures, rinv, alpha, beta)

    in_specs = (
        P("space", ("tm", "obs"), None, None, None),
        P(("groups", "space"), ("tm", "obs"), None),
        P(("groups", "tm", "obs"), None),
        P("space"),
        P(("groups", "space"), None),
        P(("groups", "tm", "obs"), "space", None, None),
        P(("groups", "tm", "obs"), "space", None),
        P("groups", None),
        P("groups", None),
    )
    out_specs = (
        P(("groups", "tm"), "space", None, None),
        P(("groups", "tm", "obs"), "space", None, None),
    )
    return jax.shard_map(shards, mesh=mesh, in_specs=in_specs, out_specs=out_specs, check_vma=False)
```

```python
import functools

import jax
import jax.numpy as jnp
from jax import lax
from jax.experimental import pallas as pl
from jax.experimental.pallas import tpu as pltpu
from jax.sharding import PartitionSpec as P

MESH = pl.DeviceIdType.MESH

TW = 2
RD = 2

OCEAN = 0.35
SPATIAL = 0.2
TEMPORAL = 0.6
BF = jnp.bfloat16
F32 = jnp.float32


def kernel(
    n, nt, fp_in, which_in, order_in, land_in, sigma_in, dep_in, rinv_in, alpha_in, beta_in,
    inc, wout, fp, which, order, land, sigma, dep, rinv, alpha, beta, loaded, fpt, spread, weights, cells, zsend, zrecv, psend, precv, osend, orecv, hsend, hrows, htime,
    zs, zr, ps, pr, os_, or_, hs, hr,
):
    s = lax.axis_index("space")
    k = lax.axis_index("tm")
    c = lax.axis_index("obs")
    cols = sigma.shape[1]
    low, high = s > 0, s < n - 1
    prev, nxt = k > 0, k < nt - 1
    both = jnp.logical_and

    loads = [pltpu.make_async_copy(src, dst, loaded.at[j]) for j, (src, dst) in enumerate((
        (sigma_in, sigma), (rinv_in, rinv), (dep_in, dep), (land_in, land), (order_in, order),
        (which_in, which), (alpha_in, alpha), (beta_in, beta), (fp_in, fp)))]
    for load in loads:
        load.start()

    hrows[...] = jnp.zeros_like(hrows)
    htime[...] = jnp.zeros_like(htime)

    barrier = pltpu.get_barrier_semaphore()
    partners = [(None, {"space": lax.rem(s + d, n)}) for d in range(1, n)]
    partners.append((None, {"obs": 1 - c}))
    partners.append((prev, {"tm": k - 1}))
    partners.append((nxt, {"tm": k + 1}))
    for sc, ds in ((low, -1), (high, 1)):
        for kc, dk in ((prev, -1), (nxt, 1)):
            partners.append((both(sc, kc), {"space": s + ds, "tm": k + dk}))

    def run_if(cond, action):
        if cond is None:
            action()
        else:
            pl.when(cond)(action)

    expected = 0
    for cond, target in partners:
        run_if(cond, functools.partial(
            pl.semaphore_signal, barrier, inc=1, device_id=target, device_id_type=MESH))
        expected = expected + (1 if cond is None else cond.astype(jnp.int32))

    for load in loads[:-1]:
        load.wait()
    scale = jnp.where(land[0] == 1, 1.0, OCEAN).astype(F32)
    for r in range(RD):
        spread[r] = jnp.broadcast_to(sigma[r:r + 1, :], (cols, cols)).T * scale
    height = weights.shape[0]
    lanes = weights.shape[1]
    for i in range(0, height, lanes):
        weights[i:i + lanes] = jnp.broadcast_to(rinv[0, :, i:i + lanes], (lanes, lanes)).T
    zsend[0] = (weights[...] * dep[0, 0]).astype(BF)

    pl.semaphore_wait(barrier, expected)
    pending = []

    def send(src, dst, ssem, rsem, target, cond=None):
        copy = pltpu.make_async_remote_copy(
            src_ref=src, dst_ref=dst, send_sem=ssem, recv_sem=rsem,
            device_id=target, device_id_type=MESH)
        run_if(cond, copy.start)
        pending.append((cond, copy))
        return copy

    def hops():
        return sorted(range(1, n), key=lambda d: -min(d, n - d))

    def gather_start(i):
        return {d: send(zsend.at[i], zrecv.at[i, d], zs.at[i, d], zr.at[i, d],
                        {"space": lax.rem(s + d, n)}) for d in hops()}

    def contribution(z, position):
        block = order[0, position]
        tile = which[0, 0, block]
        wide = z.astype(F32)
        parts = [wide * jnp.where(tile == t, 1.0, 0.0).astype(F32) for t in range(TW)]
        return jnp.dot(fpt[block], jnp.concatenate(parts, axis=1).astype(BF),
                       preferred_element_type=F32)

    def adjoint(i, copies):
        total = contribution(zsend[i], s)
        for d in reversed(hops()):
            copies[d].wait_recv()
            total = total + contribution(zrecv[i, d], lax.rem(s + n - d, n))
        for t in range(TW):
            osend[i, t] = total[:, t * lanes:(t + 1) * lanes].astype(BF)
        copy = send(osend.at[i], orecv.at[i], os_.at[i], or_.at[i], {"obs": 1 - c})
        copy.wait_recv()
        out = []
        for t in range(TW):
            tile = osend[i, t].astype(F32) + orecv[i, t].astype(F32)
            out.append([tile[r * cols:(r + 1) * cols] * spread[r] for r in range(RD)])
        return smooth(2 * i, out, False)

    def smooth(h, q, forward):
        for t in range(TW):
            for r in range(RD):
                hsend[h, t, r] = q[t][r].astype(BF)
        edge = TW - 1 if forward else 0
        step = 1 if forward else -1
        there, here = (nxt, prev) if forward else (prev, nxt)
        sides = ((high, low, 1, RD - 1, 0), (low, high, -1, 0, 1))
        waits = []
        for j, (to, frm, ds, row, side) in enumerate(sides):
            waits.append((frm, send(
                hsend.at[h, :, row], hrows.at[h, side, pl.ds(0, TW)], hs.at[h, j], hr.at[h, j],
                {"space": s + ds}, to)))
        for j, (to, frm, ds, row, side) in enumerate(sides):
            waits.append((both(frm, here), send(
                hsend.at[h, edge, row], hrows.at[h, side, TW], hs.at[h, 2 + j], hr.at[h, 2 + j],
                {"space": s + ds, "tm": k + step}, both(to, there))))
        waits.append((here, send(
            hsend.at[h, edge], htime.at[h], hs.at[h, 4], hr.at[h, 4], {"tm": k + step}, there)))
        for cond, copy in waits:
            run_if(cond, copy.wait_recv)
        at = lax.broadcasted_iota(jnp.int32, (cols, lanes), 0)
        out = []
        for t in range(TW):
            other = t - 1 if forward else t + 1
            inside = 0 <= other < TW
            slot = other if inside else TW
            rows = [hrows[h, 0, t].astype(F32) + TEMPORAL * hrows[h, 0, slot].astype(F32)]
            for r in range(RD):
                beside = q[other][r] if inside else htime[h, r].astype(F32)
                rows.append(q[t][r] + TEMPORAL * beside)
            rows.append(hrows[h, 1, t].astype(F32) + TEMPORAL * hrows[h, 1, slot].astype(F32))
            done = []
            for r in range(RD):
                u = rows[r + 1]
                left = jnp.where(at == 0, 0.0, pltpu.roll(u, 1, 0))
                right = jnp.where(at == cols - 1, 0.0, pltpu.roll(u, cols - 1, 0))
                done.append(u + SPATIAL * (rows[r] + rows[r + 2] + left + right))
            out.append(done)
        return out

    def correlate(h, field):
        done = smooth(h, field, True)
        return [[done[t][r] * spread[r] for r in range(RD)] for t in range(TW)]

    def observe(i, field):
        for t in range(TW):
            for r in range(RD):
                cells[i, t, r * cols:(r + 1) * cols] = field[t][r].astype(BF)

        def term(position):
            block = order[0, position]
            return jnp.dot(fp[0, 0, block], cells[i, which[0, 0, block]],
                           preferred_element_type=F32).astype(BF)

        copies = {}
        for d in hops():
            position = lax.rem(s + d, n)
            psend[i, d] = term(position)
            copies[d] = send(psend.at[i, d], precv.at[i, d], ps.at[i, d], pr.at[i, d],
                             {"space": position})
        total = term(s).astype(F32)
        for d in reversed(hops()):
            copies[d].wait_recv()
            total = total + precv[i, d].astype(F32)
        return total

    copies = gather_start(0)
    loads[-1].wait()
    for b in range(n):
        fpt[b] = fp[0, 0, b].T
    gradient = adjoint(0, copies)
    zsend[1] = (weights[...] * observe(0, correlate(1, gradient))).astype(BF)
    image = adjoint(1, gather_start(1))
    first, second, turn = alpha[0:1, :], alpha[1:2, :], beta[0:1, :]
    state = []
    for t in range(TW):
        rows = []
        for r in range(RD):
            g = gradient[t][r]
            residual = g - first * (g + image[t][r])
            rows.append(first * g + second * (residual + turn * g))
        state.append(rows)
    increment = correlate(3, state)
    for t in range(TW):
        for r in range(RD):
            inc[t, r] = increment[t][r]
    fitted = observe(1, increment)
    wout[0, 0] = weights[...] * (fitted - dep[0, 0])
    for cond, copy in pending:
        run_if(cond, copy.wait_send)


def solution(mesh):
    n, nt = mesh.shape["space"], mesh.shape["tm"]

    def shards(footprint, tile_index, assign, land, sigma, departures, rinv, alpha, beta):
        blocks, width = footprint.shape[2], footprint.shape[3]
        cols, members = sigma.shape[1], alpha.shape[1]
        assert blocks == n and width == RD * cols and sigma.shape[0] == RD
        vmem = pl.BlockSpec(memory_space=pltpu.VMEM)
        outside = pl.BlockSpec(memory_space=pltpu.HBM)
        operands = (footprint, tile_index, assign, land, sigma, departures, rinv, alpha, beta)
        scalars = (tile_index, assign, land)
        dma = pltpu.SemaphoreType.DMA
        return pl.pallas_call(
            functools.partial(kernel, n, nt),
            out_shape=(
                jax.ShapeDtypeStruct((TW, RD, cols, members), F32),
                jax.ShapeDtypeStruct((1, 1, width, members), F32),
            ),
            in_specs=[outside] * len(operands),
            out_specs=(vmem, vmem),
            scratch_shapes=[
                *((pltpu.SMEM if any(a is b for b in scalars) else pltpu.VMEM)(a.shape, a.dtype)
                  for a in operands),
                dma((len(operands),)),
                pltpu.VMEM((n, width, width), BF),
                pltpu.VMEM((RD, cols, members), F32),
                pltpu.VMEM((width, members), F32),
                pltpu.VMEM((2, TW, width, members), BF),
                pltpu.VMEM((2, width, members), BF),
                pltpu.VMEM((2, n, width, members), BF),
                pltpu.VMEM((2, n, width, members), BF),
                pltpu.VMEM((2, n, width, members), BF),
                pltpu.VMEM((2, TW, width, members), BF),
                pltpu.VMEM((2, TW, width, members), BF),
                pltpu.VMEM((4, TW, RD, cols, members), BF),
                pltpu.VMEM((4, 2, TW + 1, cols, members), BF),
                pltpu.VMEM((4, RD, cols, members), BF),
                dma((2, n)), dma((2, n)), dma((2, n)), dma((2, n)),
                dma((2,)), dma((2,)), dma((4, 5)), dma((4, 5)),
            ],
            compiler_params=pltpu.CompilerParams(
                collective_id=0, has_side_effects=True, vmem_limit_bytes=63 * 1024 * 1024
            ),
        )(*operands)

    in_specs = (
        P("space", ("tm", "obs"), None, None, None),
        P(("groups", "space"), ("tm", "obs"), None),
        P(("groups", "tm", "obs"), None),
        P("space"),
        P(("groups", "space"), None),
        P(("groups", "tm", "obs"), "space", None, None),
        P(("groups", "tm", "obs"), "space", None),
        P("groups", None),
        P("groups", None),
    )
    out_specs = (
        P(("groups", "tm"), "space", None, None),
        P(("groups", "tm", "obs"), "space", None, None),
    )
    return jax.shard_map(shards, mesh=mesh, in_specs=in_specs, out_specs=out_specs, check_vma=False)
```

```python
import functools

import jax
import jax.numpy as jnp
from jax import lax
from jax.experimental import pallas as pl
from jax.experimental.pallas import tpu as pltpu
from jax.sharding import PartitionSpec as P

MESH = pl.DeviceIdType.MESH

TW = 2
RD = 2

OCEAN = 0.35
SPATIAL = 0.2
TEMPORAL = 0.6
BF = jnp.bfloat16
F32 = jnp.float32


def kernel(
    n, nt, fp_in, which_in, order_in, land_in, sigma_in, dep_in, rinv_in, alpha_in, beta_in,
    inc, wout, fp, which, order, land, sigma, dep, rinv, alpha, beta, loaded, fpt, spread, weights, cells, zsend, zrecv, psend, precv, osend, orecv, hsend, hrows, htime, part,
    zs, zr, ps, pr, os_, or_, hs, hr,
):
    s = lax.axis_index("space")
    k = lax.axis_index("tm")
    c = lax.axis_index("obs")
    cols = sigma.shape[1]
    low, high = s > 0, s < n - 1
    prev, nxt = k > 0, k < nt - 1
    both = jnp.logical_and
    relay = n == 4

    loads = [pltpu.make_async_copy(src, dst, loaded.at[j]) for j, (src, dst) in enumerate((
        (sigma_in, sigma), (rinv_in, rinv), (dep_in, dep), (land_in, land), (order_in, order),
        (which_in, which), (alpha_in, alpha), (beta_in, beta), (fp_in, fp)))]
    for load in loads:
        load.start()

    hrows[...] = jnp.zeros_like(hrows)
    htime[...] = jnp.zeros_like(htime)

    barrier = pltpu.get_barrier_semaphore()
    partners = [(None, {"space": lax.rem(s + d, n)}) for d in range(1, n)]
    partners.append((None, {"obs": 1 - c}))
    partners.append((prev, {"tm": k - 1}))
    partners.append((nxt, {"tm": k + 1}))
    for sc, ds in ((low, -1), (high, 1)):
        for kc, dk in ((prev, -1), (nxt, 1)):
            partners.append((both(sc, kc), {"space": s + ds, "tm": k + dk}))

    def run_if(cond, action):
        if cond is None:
            action()
        else:
            pl.when(cond)(action)

    expected = 0
    for cond, target in partners:
        run_if(cond, functools.partial(
            pl.semaphore_signal, barrier, inc=1, device_id=target, device_id_type=MESH))
        expected = expected + (1 if cond is None else cond.astype(jnp.int32))

    for load in loads[:-1]:
        load.wait()
    scale = jnp.where(land[0] == 1, 1.0, OCEAN).astype(F32)
    for r in range(RD):
        spread[r] = jnp.broadcast_to(sigma[r:r + 1, :], (cols, cols)).T * scale
    height = weights.shape[0]
    lanes = weights.shape[1]
    for i in range(0, height, lanes):
        weights[i:i + lanes] = jnp.broadcast_to(rinv[0, :, i:i + lanes], (lanes, lanes)).T
    zsend[0] = (weights[...] * dep[0, 0]).astype(BF)

    pl.semaphore_wait(barrier, expected)
    pending = []

    def send(src, dst, ssem, rsem, target, cond=None):
        copy = pltpu.make_async_remote_copy(
            src_ref=src, dst_ref=dst, send_sem=ssem, recv_sem=rsem,
            device_id=target, device_id_type=MESH)
        run_if(cond, copy.start)
        pending.append((cond, copy))
        return copy

    def hops():
        return sorted(range(1, n), key=lambda d: -min(d, n - d))

    def gather_start(i):
        copies = {}
        for d in hops():
            copies[d] = (ends_only if relay and d == 2 else send)(
                zsend.at[i], zrecv.at[i, d], zs.at[i, d], zr.at[i, d],
                {"space": lax.rem(s + d, n)})
        return copies

    def ends_only(src, dst, ssem, rsem, target):
        at_end = jnp.logical_or(s == 0, s == n - 1)
        return send(src, dst, ssem, rsem, target, at_end)

    def pass_on(i, d):
        if not relay or d == 2:
            return
        target = 3 if d == 1 else 0
        send(zrecv.at[i, d], zrecv.at[i, 2], zs.at[i, 2], zr.at[i, 2], {"space": target},
             s == (2 if d == 1 else 1))

    def contribution(z, position):
        block = order[0, position]
        tile = which[0, 0, block]
        wide = z.astype(F32)
        parts = [wide * jnp.where(tile == t, 1.0, 0.0).astype(F32) for t in range(TW)]
        return jnp.dot(fpt[block], jnp.concatenate(parts, axis=1).astype(BF),
                       preferred_element_type=F32)

    def adjoint(i, copies):
        total = contribution(zsend[i], s)
        early = [d for d in reversed(hops()) if relay and d != 2]
        for d in early:
            copies[d].wait_recv()
            pass_on(i, d)
        for d in reversed(hops()):
            if d not in early:
                copies[d].wait_recv()
            total = total + contribution(zrecv[i, d], lax.rem(s + n - d, n))
        for t in range(TW):
            osend[i, t] = total[:, t * lanes:(t + 1) * lanes].astype(BF)
        copy = send(osend.at[i], orecv.at[i], os_.at[i], or_.at[i], {"obs": 1 - c})
        copy.wait_recv()
        out = []
        for t in range(TW):
            tile = osend[i, t].astype(F32) + orecv[i, t].astype(F32)
            out.append([tile[r * cols:(r + 1) * cols] * spread[r] for r in range(RD)])
        return smooth(2 * i, out, False)

    def smooth(h, q, forward):
        for t in range(TW):
            for r in range(RD):
                hsend[h, t, r] = q[t][r].astype(BF)
        edge = TW - 1 if forward else 0
        step = 1 if forward else -1
        there, here = (nxt, prev) if forward else (prev, nxt)
        sides = ((high, low, 1, RD - 1, 0), (low, high, -1, 0, 1))
        waits = []
        for j, (to, frm, ds, row, side) in enumerate(sides):
            waits.append((both(frm, here), send(
                hsend.at[h, edge, row], hrows.at[h, side, TW], hs.at[h, 2 + j], hr.at[h, 2 + j],
                {"space": s + ds, "tm": k + step}, both(to, there))))
        last = (here, send(
            hsend.at[h, edge], htime.at[h], hs.at[h, 4], hr.at[h, 4], {"tm": k + step}, there))
        for j, (to, frm, ds, row, side) in enumerate(sides):
            waits.append((frm, send(
                hsend.at[h, :, row], hrows.at[h, side, pl.ds(0, TW)], hs.at[h, j], hr.at[h, j],
                {"space": s + ds}, to)))
        at = lax.broadcasted_iota(jnp.int32, (cols, lanes), 0)
        other = [t - 1 if forward else t + 1 for t in range(TW)]
        inside = [0 <= o < TW for o in other]

        def own(t):
            us = []
            for r in range(RD):
                beside = q[other[t]][r] if inside[t] else htime[h, r].astype(F32)
                us.append(q[t][r] + TEMPORAL * beside)
            for r in range(RD):
                u = us[r]
                total = jnp.where(at == 0, 0.0, pltpu.roll(u, 1, 0))
                total = total + jnp.where(at == cols - 1, 0.0, pltpu.roll(u, cols - 1, 0))
                for near in (r - 1, r + 1):
                    if 0 <= near < RD:
                        total = total + us[near]
                part[t, r] = u + SPATIAL * total

        for t in range(TW):
            if inside[t]:
                own(t)
        run_if(last[0], last[1].wait_recv)
        for t in range(TW):
            if not inside[t]:
                own(t)
        for cond, copy in waits:
            run_if(cond, copy.wait_recv)
        out = []
        for t in range(TW):
            slot = other[t] if inside[t] else TW
            done = [part[t, r] for r in range(RD)]
            for side, r in ((0, 0), (1, RD - 1)):
                beyond = hrows[h, side, t].astype(F32) + TEMPORAL * hrows[h, side, slot].astype(F32)
                done[r] = done[r] + SPATIAL * beyond
            out.append(done)
        return out

    def correlate(h, field):
        done = smooth(h, field, True)
        return [[done[t][r] * spread[r] for r in range(RD)] for t in range(TW)]

    def observe(i, field):
        for t in range(TW):
            for r in range(RD):
                cells[i, t, r * cols:(r + 1) * cols] = field[t][r].astype(BF)

        def term(position):
            block = order[0, position]
            return jnp.dot(fp[0, 0, block], cells[i, which[0, 0, block]],
                           preferred_element_type=F32).astype(BF)

        copies = {}
        for d in hops():
            position = lax.rem(s + d, n)
            psend[i, d] = term(position)
            copies[d] = send(psend.at[i, d], precv.at[i, d], ps.at[i, d], pr.at[i, d],
                             {"space": position})
        total = term(s).astype(F32)
        for d in reversed(hops()):
            copies[d].wait_recv()
            total = total + precv[i, d].astype(F32)
        return total

    copies = gather_start(0)
    loads[-1].wait()
    for b in range(n):
        fpt[b] = fp[0, 0, b].T
    gradient = adjoint(0, copies)
    zsend[1] = (weights[...] * observe(0, correlate(1, gradient))).astype(BF)
    image = adjoint(1, gather_start(1))
    first, second, turn = alpha[0:1, :], alpha[1:2, :], beta[0:1, :]
    state = []
    for t in range(TW):
        rows = []
        for r in range(RD):
            g = gradient[t][r]
            residual = g - first * (g + image[t][r])
            rows.append(first * g + second * (residual + turn * g))
        state.append(rows)
    increment = correlate(3, state)
    for t in range(TW):
        for r in range(RD):
            inc[t, r] = increment[t][r]
    fitted = observe(1, increment)
    wout[0, 0] = weights[...] * (fitted - dep[0, 0])
    for cond, copy in pending:
        run_if(cond, copy.wait_send)


def solution(mesh):
    n, nt = mesh.shape["space"], mesh.shape["tm"]

    def shards(footprint, tile_index, assign, land, sigma, departures, rinv, alpha, beta):
        blocks, width = footprint.shape[2], footprint.shape[3]
        cols, members = sigma.shape[1], alpha.shape[1]
        assert blocks == n and width == RD * cols and sigma.shape[0] == RD
        vmem = pl.BlockSpec(memory_space=pltpu.VMEM)
        outside = pl.BlockSpec(memory_space=pltpu.HBM)
        operands = (footprint, tile_index, assign, land, sigma, departures, rinv, alpha, beta)
        scalars = (tile_index, assign, land)
        dma = pltpu.SemaphoreType.DMA
        return pl.pallas_call(
            functools.partial(kernel, n, nt),
            out_shape=(
                jax.ShapeDtypeStruct((TW, RD, cols, members), F32),
                jax.ShapeDtypeStruct((1, 1, width, members), F32),
            ),
            in_specs=[outside] * len(operands),
            out_specs=(vmem, vmem),
            scratch_shapes=[
                *((pltpu.SMEM if any(a is b for b in scalars) else pltpu.VMEM)(a.shape, a.dtype)
                  for a in operands),
                dma((len(operands),)),
                pltpu.VMEM((n, width, width), BF),
                pltpu.VMEM((RD, cols, members), F32),
                pltpu.VMEM((width, members), F32),
                pltpu.VMEM((2, TW, width, members), BF),
                pltpu.VMEM((2, width, members), BF),
                pltpu.VMEM((2, n, width, members), BF),
                pltpu.VMEM((2, n, width, members), BF),
                pltpu.VMEM((2, n, width, members), BF),
                pltpu.VMEM((2, TW, width, members), BF),
                pltpu.VMEM((2, TW, width, members), BF),
                pltpu.VMEM((4, TW, RD, cols, members), BF),
                pltpu.VMEM((4, 2, TW + 1, cols, members), BF),
                pltpu.VMEM((4, RD, cols, members), BF),
                pltpu.VMEM((TW, RD, cols, members), F32),
                dma((2, n)), dma((2, n)), dma((2, n)), dma((2, n)),
                dma((2,)), dma((2,)), dma((4, 5)), dma((4, 5)),
            ],
            compiler_params=pltpu.CompilerParams(
                collective_id=0, has_side_effects=True, vmem_limit_bytes=63 * 1024 * 1024
            ),
        )(*operands)

    in_specs = (
        P("space", ("tm", "obs"), None, None, None),
        P(("groups", "space"), ("tm", "obs"), None),
        P(("groups", "tm", "obs"), None),
        P("space"),
        P(("groups", "space"), None),
        P(("groups", "tm", "obs"), "space", None, None),
        P(("groups", "tm", "obs"), "space", None),
        P("groups", None),
        P("groups", None),
    )
    out_specs = (
        P(("groups", "tm"), "space", None, None),
        P(("groups", "tm", "obs"), "space", None, None),
    )
    return jax.shard_map(shards, mesh=mesh, in_specs=in_specs, out_specs=out_specs, check_vma=False)
```

```python
import functools

import jax
import jax.numpy as jnp
from jax import lax
from jax.experimental import pallas as pl
from jax.experimental.pallas import tpu as pltpu
from jax.sharding import PartitionSpec as P

MESH = pl.DeviceIdType.MESH

TW = 2
RD = 2

OCEAN = 0.35
SPATIAL = 0.2
TEMPORAL = 0.6
BF = jnp.bfloat16
F32 = jnp.float32


def kernel(
    n, nt, fp_in, which_in, order_in, land_in, sigma_in, dep_in, rinv_in, alpha_in, beta_in,
    inc_out, w_out, inc, wout, stored, fp, which, order, land, sigma, dep, rinv, alpha, beta, loaded, fpt, spread, weights, cells, zsend, zrecv, psend, precv, osend, orecv, hsend, hrows, htime, part,
    zs, zr, ps, pr, os_, or_, hs, hr,
):
    s = lax.axis_index("space")
    k = lax.axis_index("tm")
    c = lax.axis_index("obs")
    cols = sigma.shape[1]
    low, high = s > 0, s < n - 1
    prev, nxt = k > 0, k < nt - 1
    both = jnp.logical_and

    loads = [pltpu.make_async_copy(src, dst, loaded.at[j]) for j, (src, dst) in enumerate((
        (sigma_in, sigma), (rinv_in, rinv), (dep_in, dep), (land_in, land), (order_in, order),
        (which_in, which), (alpha_in, alpha), (beta_in, beta), (fp_in, fp)))]
    for load in loads:
        load.start()

    hrows[...] = jnp.zeros_like(hrows)
    htime[...] = jnp.zeros_like(htime)

    barrier = pltpu.get_barrier_semaphore()
    partners = [(None, {"space": lax.rem(s + d, n)}) for d in range(1, n)]
    partners.append((None, {"obs": 1 - c}))
    partners.append((prev, {"tm": k - 1}))
    partners.append((nxt, {"tm": k + 1}))
    for sc, ds in ((low, -1), (high, 1)):
        for kc, dk in ((prev, -1), (nxt, 1)):
            partners.append((both(sc, kc), {"space": s + ds, "tm": k + dk}))

    def run_if(cond, action):
        if cond is None:
            action()
        else:
            pl.when(cond)(action)

    expected = 0
    for cond, target in partners:
        run_if(cond, functools.partial(
            pl.semaphore_signal, barrier, inc=1, device_id=target, device_id_type=MESH))
        expected = expected + (1 if cond is None else cond.astype(jnp.int32))

    for load in loads[:-1]:
        load.wait()
    scale = jnp.where(land[0] == 1, 1.0, OCEAN).astype(F32)
    for r in range(RD):
        spread[r] = jnp.broadcast_to(sigma[r:r + 1, :], (cols, cols)).T * scale
    height = weights.shape[0]
    lanes = weights.shape[1]
    for i in range(0, height, lanes):
        weights[i:i + lanes] = jnp.broadcast_to(rinv[0, :, i:i + lanes], (lanes, lanes)).T
    zsend[0] = (weights[...] * dep[0, 0]).astype(BF)

    pl.semaphore_wait(barrier, expected)
    pending = []

    def send(src, dst, ssem, rsem, target, cond=None):
        copy = pltpu.make_async_remote_copy(
            src_ref=src, dst_ref=dst, send_sem=ssem, recv_sem=rsem,
            device_id=target, device_id_type=MESH)
        run_if(cond, copy.start)
        pending.append((cond, copy))
        return copy

    def hops():
        return sorted(range(1, n), key=lambda d: -min(d, n - d))

    def gather_start(i):
        return {d: send(zsend.at[i], zrecv.at[i, d], zs.at[i, d], zr.at[i, d],
                        {"space": lax.rem(s + d, n)}) for d in hops()}

    def contribution(z, position):
        block = order[0, position]
        tile = which[0, 0, block]
        wide = z.astype(F32)
        parts = [wide * jnp.where(tile == t, 1.0, 0.0).astype(F32) for t in range(TW)]
        return jnp.dot(fpt[block], jnp.concatenate(parts, axis=1).astype(BF),
                       preferred_element_type=F32)

    def adjoint(i, copies):
        total = contribution(zsend[i], s)
        for d in reversed(hops()):
            copies[d].wait_recv()
            total = total + contribution(zrecv[i, d], lax.rem(s + n - d, n))
        for t in range(TW):
            osend[i, t] = total[:, t * lanes:(t + 1) * lanes].astype(BF)
        copy = send(osend.at[i], orecv.at[i], os_.at[i], or_.at[i], {"obs": 1 - c})
        copy.wait_recv()
        out = []
        for t in range(TW):
            tile = osend[i, t].astype(F32) + orecv[i, t].astype(F32)
            out.append([tile[r * cols:(r + 1) * cols] * spread[r] for r in range(RD)])
        return smooth(2 * i, out, False)

    def smooth(h, q, forward):
        for t in range(TW):
            for r in range(RD):
                hsend[h, t, r] = q[t][r].astype(BF)
        edge = TW - 1 if forward else 0
        step = 1 if forward else -1
        there, here = (nxt, prev) if forward else (prev, nxt)
        sides = ((high, low, 1, RD - 1, 0), (low, high, -1, 0, 1))
        waits = []
        for j, (to, frm, ds, row, side) in enumerate(sides):
            waits.append((both(frm, here), send(
                hsend.at[h, edge, row], hrows.at[h, side, TW], hs.at[h, 2 + j], hr.at[h, 2 + j],
                {"space": s + ds, "tm": k + step}, both(to, there))))
        last = (here, send(
            hsend.at[h, edge], htime.at[h], hs.at[h, 4], hr.at[h, 4], {"tm": k + step}, there))
        for j, (to, frm, ds, row, side) in enumerate(sides):
            waits.append((frm, send(
                hsend.at[h, :, row], hrows.at[h, side, pl.ds(0, TW)], hs.at[h, j], hr.at[h, j],
                {"space": s + ds}, to)))
        at = lax.broadcasted_iota(jnp.int32, (cols, lanes), 0)
        other = [t - 1 if forward else t + 1 for t in range(TW)]
        inside = [0 <= o < TW for o in other]

        def own(t):
            us = []
            for r in range(RD):
                beside = q[other[t]][r] if inside[t] else htime[h, r].astype(F32)
                us.append(q[t][r] + TEMPORAL * beside)
            for r in range(RD):
                u = us[r]
                total = jnp.where(at == 0, 0.0, pltpu.roll(u, 1, 0))
                total = total + jnp.where(at == cols - 1, 0.0, pltpu.roll(u, cols - 1, 0))
                for near in (r - 1, r + 1):
                    if 0 <= near < RD:
                        total = total + us[near]
                part[t, r] = u + SPATIAL * total

        for t in range(TW):
            if inside[t]:
                own(t)
        run_if(last[0], last[1].wait_recv)
        for t in range(TW):
            if not inside[t]:
                own(t)
        for cond, copy in waits:
            run_if(cond, copy.wait_recv)
        out = []
        for t in range(TW):
            slot = other[t] if inside[t] else TW
            done = [part[t, r] for r in range(RD)]
            for side, r in ((0, 0), (1, RD - 1)):
                beyond = hrows[h, side, t].astype(F32) + TEMPORAL * hrows[h, side, slot].astype(F32)
                done[r] = done[r] + SPATIAL * beyond
            out.append(done)
        return out

    def correlate(h, field):
        done = smooth(h, field, True)
        return [[done[t][r] * spread[r] for r in range(RD)] for t in range(TW)]

    def observe(i, field):
        for t in range(TW):
            for r in range(RD):
                cells[i, t, r * cols:(r + 1) * cols] = field[t][r].astype(BF)

        def term(position):
            block = order[0, position]
            return jnp.dot(fp[0, 0, block], cells[i, which[0, 0, block]],
                           preferred_element_type=F32).astype(BF)

        copies = {}
        for d in hops():
            position = lax.rem(s + d, n)
            psend[i, d] = term(position)
            copies[d] = send(psend.at[i, d], precv.at[i, d], ps.at[i, d], pr.at[i, d],
                             {"space": position})
        total = term(s).astype(F32)
        for d in reversed(hops()):
            copies[d].wait_recv()
            total = total + precv[i, d].astype(F32)
        return total

    copies = gather_start(0)
    loads[-1].wait()
    for b in range(n):
        fpt[b] = fp[0, 0, b].T
    gradient = adjoint(0, copies)
    zsend[1] = (weights[...] * observe(0, correlate(1, gradient))).astype(BF)
    image = adjoint(1, gather_start(1))
    first, second, turn = alpha[0:1, :], alpha[1:2, :], beta[0:1, :]
    state = []
    for t in range(TW):
        rows = []
        for r in range(RD):
            g = gradient[t][r]
            residual = g - first * (g + image[t][r])
            rows.append(first * g + second * (residual + turn * g))
        state.append(rows)
    increment = correlate(3, state)
    for t in range(TW):
        for r in range(RD):
            inc[t, r] = increment[t][r]
    inc_copy = pltpu.make_async_copy(inc, inc_out, stored.at[0])
    inc_copy.start()
    fitted = observe(1, increment)
    wout[0, 0] = weights[...] * (fitted - dep[0, 0])
    w_copy = pltpu.make_async_copy(wout, w_out, stored.at[1])
    w_copy.start()
    inc_copy.wait()
    w_copy.wait()
    for cond, copy in pending:
        run_if(cond, copy.wait_send)


def solution(mesh):
    n, nt = mesh.shape["space"], mesh.shape["tm"]

    def shards(footprint, tile_index, assign, land, sigma, departures, rinv, alpha, beta):
        blocks, width = footprint.shape[2], footprint.shape[3]
        cols, members = sigma.shape[1], alpha.shape[1]
        assert blocks == n and width == RD * cols and sigma.shape[0] == RD
        outside = pl.BlockSpec(memory_space=pltpu.HBM)
        operands = (footprint, tile_index, assign, land, sigma, departures, rinv, alpha, beta)
        scalars = (tile_index, assign, land)
        dma = pltpu.SemaphoreType.DMA
        return pl.pallas_call(
            functools.partial(kernel, n, nt),
            out_shape=(
                jax.ShapeDtypeStruct((TW, RD, cols, members), F32),
                jax.ShapeDtypeStruct((1, 1, width, members), F32),
            ),
            in_specs=[outside] * len(operands),
            out_specs=(outside, outside),
            scratch_shapes=[
                pltpu.VMEM((TW, RD, cols, members), F32),
                pltpu.VMEM((1, 1, width, members), F32),
                dma((2,)),
                *((pltpu.SMEM if any(a is b for b in scalars) else pltpu.VMEM)(a.shape, a.dtype)
                  for a in operands),
                dma((len(operands),)),
                pltpu.VMEM((n, width, width), BF),
                pltpu.VMEM((RD, cols, members), F32),
                pltpu.VMEM((width, members), F32),
                pltpu.VMEM((2, TW, width, members), BF),
                pltpu.VMEM((2, width, members), BF),
                pltpu.VMEM((2, n, width, members), BF),
                pltpu.VMEM((2, n, width, members), BF),
                pltpu.VMEM((2, n, width, members), BF),
                pltpu.VMEM((2, TW, width, members), BF),
                pltpu.VMEM((2, TW, width, members), BF),
                pltpu.VMEM((4, TW, RD, cols, members), BF),
                pltpu.VMEM((4, 2, TW + 1, cols, members), BF),
                pltpu.VMEM((4, RD, cols, members), BF),
                pltpu.VMEM((TW, RD, cols, members), F32),
                dma((2, n)), dma((2, n)), dma((2, n)), dma((2, n)),
                dma((2,)), dma((2,)), dma((4, 5)), dma((4, 5)),
            ],
            compiler_params=pltpu.CompilerParams(
                collective_id=0, has_side_effects=True, vmem_limit_bytes=63 * 1024 * 1024
            ),
        )(*operands)

    in_specs = (
        P("space", ("tm", "obs"), None, None, None),
        P(("groups", "space"), ("tm", "obs"), None),
        P(("groups", "tm", "obs"), None),
        P("space"),
        P(("groups", "space"), None),
        P(("groups", "tm", "obs"), "space", None, None),
        P(("groups", "tm", "obs"), "space", None),
        P("groups", None),
        P("groups", None),
    )
    out_specs = (
        P(("groups", "tm"), "space", None, None),
        P(("groups", "tm", "obs"), "space", None, None),
    )
    return jax.shard_map(shards, mesh=mesh, in_specs=in_specs, out_specs=out_specs, check_vma=False)
```

```python
import functools

import jax
import jax.numpy as jnp
from jax import lax
from jax.experimental import pallas as pl
from jax.experimental.pallas import tpu as pltpu
from jax.sharding import PartitionSpec as P

MESH = pl.DeviceIdType.MESH

TW = 2
RD = 2

OCEAN = 0.35
SPATIAL = 0.2
TEMPORAL = 0.6
BF = jnp.bfloat16
F32 = jnp.float32


def kernel(
    n, nt, fp_in, which_in, order_in, land_in, sigma_in, dep_in, rinv_in, alpha_in, beta_in,
    inc_out, w_out, inc, wout, stored, fp, which, order, land, sigma, dep, rinv, alpha, beta, loaded, fpt, spread, weights, cells, zsend, zrecv, psend, precv, osend, orecv, hsend, hrows, htime, part,
    zs, zr, ps, pr, os_, or_, hs, hr,
):
    s = lax.axis_index("space")
    k = lax.axis_index("tm")
    c = lax.axis_index("obs")
    cols = sigma.shape[1]
    low, high = s > 0, s < n - 1
    prev, nxt = k > 0, k < nt - 1
    both = jnp.logical_and

    loads = [pltpu.make_async_copy(src, dst, loaded.at[j]) for j, (src, dst) in enumerate((
        (sigma_in, sigma), (rinv_in, rinv), (dep_in, dep), (land_in, land), (order_in, order),
        (which_in, which), (alpha_in, alpha), (beta_in, beta), (fp_in, fp)))]
    for load in loads:
        load.start()

    hrows[...] = jnp.zeros_like(hrows)
    htime[...] = jnp.zeros_like(htime)

    barrier = pltpu.get_barrier_semaphore()
    partners = [(None, {"space": lax.rem(s + d, n)}) for d in range(1, n)]
    partners.append((None, {"obs": 1 - c}))
    partners.append((prev, {"tm": k - 1}))
    partners.append((nxt, {"tm": k + 1}))
    for sc, ds in ((low, -1), (high, 1)):
        for kc, dk in ((prev, -1), (nxt, 1)):
            partners.append((both(sc, kc), {"space": s + ds, "tm": k + dk}))

    def run_if(cond, action):
        if cond is None:
            action()
        else:
            pl.when(cond)(action)

    expected = 0
    for cond, target in partners:
        run_if(cond, functools.partial(
            pl.semaphore_signal, barrier, inc=1, device_id=target, device_id_type=MESH))
        expected = expected + (1 if cond is None else cond.astype(jnp.int32))

    for load in loads[:-1]:
        load.wait()
    scale = jnp.where(land[0] == 1, 1.0, OCEAN).astype(F32)
    for r in range(RD):
        spread[r] = jnp.broadcast_to(sigma[r:r + 1, :], (cols, cols)).T * scale
    height = weights.shape[0]
    lanes = weights.shape[1]
    for i in range(0, height, lanes):
        weights[i:i + lanes] = jnp.broadcast_to(rinv[0, :, i:i + lanes], (lanes, lanes)).T
    zsend[0] = (weights[...] * dep[0, 0]).astype(BF)

    pl.semaphore_wait(barrier, expected)
    pending = []

    def send(src, dst, ssem, rsem, target, cond=None):
        copy = pltpu.make_async_remote_copy(
            src_ref=src, dst_ref=dst, send_sem=ssem, recv_sem=rsem,
            device_id=target, device_id_type=MESH)
        run_if(cond, copy.start)
        pending.append((cond, copy))
        return copy

    def hops():
        return sorted(range(1, n), key=lambda d: -min(d, n - d))

    def gather_start(i):
        return {d: send(zsend.at[i], zrecv.at[i, d], zs.at[i, d], zr.at[i, d],
                        {"space": lax.rem(s + d, n)}) for d in hops()}

    def contribution(z, position):
        block = order[0, position]
        tile = which[0, 0, block]
        wide = z.astype(F32)
        parts = [wide * jnp.where(tile == t, 1.0, 0.0).astype(F32) for t in range(TW)]
        return jnp.dot(fpt[block], jnp.concatenate(parts, axis=1).astype(BF),
                       preferred_element_type=F32)

    def adjoint(i, copies):
        total = contribution(zsend[i], s)
        for d in reversed(hops()):
            copies[d].wait_recv()
            total = total + contribution(zrecv[i, d], lax.rem(s + n - d, n))
        swaps = []
        for t in range(TW):
            osend[i, t] = total[:, t * lanes:(t + 1) * lanes].astype(BF)
            swaps.append(send(osend.at[i, t], orecv.at[i, t], os_.at[i, t], or_.at[i, t],
                              {"obs": 1 - c}))

        def summed(t):
            swaps[t].wait_recv()
            tile = osend[i, t].astype(F32) + orecv[i, t].astype(F32)
            return [tile[r * cols:(r + 1) * cols] * spread[r] for r in range(RD)]

        return smooth(2 * i, summed, False)

    def smooth(h, fetch, forward):
        q = {}

        def stage(t):
            q[t] = fetch(t)
            for r in range(RD):
                hsend[h, t, r] = q[t][r].astype(BF)

        edge = TW - 1 if forward else 0
        step = 1 if forward else -1
        there, here = (nxt, prev) if forward else (prev, nxt)
        sides = ((high, low, 1, RD - 1, 0), (low, high, -1, 0, 1))
        waits = []
        stage(edge)
        for j, (to, frm, ds, row, side) in enumerate(sides):
            waits.append((both(frm, here), send(
                hsend.at[h, edge, row], hrows.at[h, side, TW], hs.at[h, 2 + j], hr.at[h, 2 + j],
                {"space": s + ds, "tm": k + step}, both(to, there))))
        last = (here, send(
            hsend.at[h, edge], htime.at[h], hs.at[h, 4], hr.at[h, 4], {"tm": k + step}, there))
        for t in range(TW):
            if t != edge:
                stage(t)
        for j, (to, frm, ds, row, side) in enumerate(sides):
            waits.append((frm, send(
                hsend.at[h, :, row], hrows.at[h, side, pl.ds(0, TW)], hs.at[h, j], hr.at[h, j],
                {"space": s + ds}, to)))
        at = lax.broadcasted_iota(jnp.int32, (cols, lanes), 0)
        other = [t - 1 if forward else t + 1 for t in range(TW)]
        inside = [0 <= o < TW for o in other]

        def own(t):
            us = []
            for r in range(RD):
                beside = q[other[t]][r] if inside[t] else htime[h, r].astype(F32)
                us.append(q[t][r] + TEMPORAL * beside)
            for r in range(RD):
                u = us[r]
                total = jnp.where(at == 0, 0.0, pltpu.roll(u, 1, 0))
                total = total + jnp.where(at == cols - 1, 0.0, pltpu.roll(u, cols - 1, 0))
                for near in (r - 1, r + 1):
                    if 0 <= near < RD:
                        total = total + us[near]
                part[t, r] = u + SPATIAL * total

        for t in range(TW):
            if inside[t]:
                own(t)
        run_if(last[0], last[1].wait_recv)
        for t in range(TW):
            if not inside[t]:
                own(t)
        for cond, copy in waits:
            run_if(cond, copy.wait_recv)
        out = []
        for t in range(TW):
            slot = other[t] if inside[t] else TW
            done = [part[t, r] for r in range(RD)]
            for side, r in ((0, 0), (1, RD - 1)):
                beyond = hrows[h, side, t].astype(F32) + TEMPORAL * hrows[h, side, slot].astype(F32)
                done[r] = done[r] + SPATIAL * beyond
            out.append(done)
        return out

    def correlate(h, field):
        done = smooth(h, field.__getitem__, True)
        return [[done[t][r] * spread[r] for r in range(RD)] for t in range(TW)]

    def observe(i, field):
        for t in range(TW):
            for r in range(RD):
                cells[i, t, r * cols:(r + 1) * cols] = field[t][r].astype(BF)

        def term(position):
            block = order[0, position]
            return jnp.dot(fp[0, 0, block], cells[i, which[0, 0, block]],
                           preferred_element_type=F32).astype(BF)

        copies = {}
        for d in hops():
            position = lax.rem(s + d, n)
            psend[i, d] = term(position)
            copies[d] = send(psend.at[i, d], precv.at[i, d], ps.at[i, d], pr.at[i, d],
                             {"space": position})
        total = term(s).astype(F32)
        for d in reversed(hops()):
            copies[d].wait_recv()
            total = total + precv[i, d].astype(F32)
        return total

    copies = gather_start(0)
    loads[-1].wait()
    for b in range(n):
        fpt[b] = fp[0, 0, b].T
    gradient = adjoint(0, copies)
    zsend[1] = (weights[...] * observe(0, correlate(1, gradient))).astype(BF)
    image = adjoint(1, gather_start(1))
    first, second, turn = alpha[0:1, :], alpha[1:2, :], beta[0:1, :]
    state = []
    for t in range(TW):
        rows = []
        for r in range(RD):
            g = gradient[t][r]
            residual = g - first * (g + image[t][r])
            rows.append(first * g + second * (residual + turn * g))
        state.append(rows)
    increment = correlate(3, state)
    for t in range(TW):
        for r in range(RD):
            inc[t, r] = increment[t][r]
    inc_copy = pltpu.make_async_copy(inc, inc_out, stored.at[0])
    inc_copy.start()
    fitted = observe(1, increment)
    wout[0, 0] = weights[...] * (fitted - dep[0, 0])
    w_copy = pltpu.make_async_copy(wout, w_out, stored.at[1])
    w_copy.start()
    inc_copy.wait()
    w_copy.wait()
    for cond, copy in pending:
        run_if(cond, copy.wait_send)


def solution(mesh):
    n, nt = mesh.shape["space"], mesh.shape["tm"]

    def shards(footprint, tile_index, assign, land, sigma, departures, rinv, alpha, beta):
        blocks, width = footprint.shape[2], footprint.shape[3]
        cols, members = sigma.shape[1], alpha.shape[1]
        assert blocks == n and width == RD * cols and sigma.shape[0] == RD
        outside = pl.BlockSpec(memory_space=pltpu.HBM)
        operands = (footprint, tile_index, assign, land, sigma, departures, rinv, alpha, beta)
        scalars = (tile_index, assign, land)
        dma = pltpu.SemaphoreType.DMA
        return pl.pallas_call(
            functools.partial(kernel, n, nt),
            out_shape=(
                jax.ShapeDtypeStruct((TW, RD, cols, members), F32),
                jax.ShapeDtypeStruct((1, 1, width, members), F32),
            ),
            in_specs=[outside] * len(operands),
            out_specs=(outside, outside),
            scratch_shapes=[
                pltpu.VMEM((TW, RD, cols, members), F32),
                pltpu.VMEM((1, 1, width, members), F32),
                dma((2,)),
                *((pltpu.SMEM if any(a is b for b in scalars) else pltpu.VMEM)(a.shape, a.dtype)
                  for a in operands),
                dma((len(operands),)),
                pltpu.VMEM((n, width, width), BF),
                pltpu.VMEM((RD, cols, members), F32),
                pltpu.VMEM((width, members), F32),
                pltpu.VMEM((2, TW, width, members), BF),
                pltpu.VMEM((2, width, members), BF),
                pltpu.VMEM((2, n, width, members), BF),
                pltpu.VMEM((2, n, width, members), BF),
                pltpu.VMEM((2, n, width, members), BF),
                pltpu.VMEM((2, TW, width, members), BF),
                pltpu.VMEM((2, TW, width, members), BF),
                pltpu.VMEM((4, TW, RD, cols, members), BF),
                pltpu.VMEM((4, 2, TW + 1, cols, members), BF),
                pltpu.VMEM((4, RD, cols, members), BF),
                pltpu.VMEM((TW, RD, cols, members), F32),
                dma((2, n)), dma((2, n)), dma((2, n)), dma((2, n)),
                dma((2, TW)), dma((2, TW)), dma((4, 5)), dma((4, 5)),
            ],
            compiler_params=pltpu.CompilerParams(
                collective_id=0, has_side_effects=True, vmem_limit_bytes=63 * 1024 * 1024
            ),
        )(*operands)

    in_specs = (
        P("space", ("tm", "obs"), None, None, None),
        P(("groups", "space"), ("tm", "obs"), None),
        P(("groups", "tm", "obs"), None),
        P("space"),
        P(("groups", "space"), None),
        P(("groups", "tm", "obs"), "space", None, None),
        P(("groups", "tm", "obs"), "space", None),
        P("groups", None),
        P("groups", None),
    )
    out_specs = (
        P(("groups", "tm"), "space", None, None),
        P(("groups", "tm", "obs"), "space", None, None),
    )
    return jax.shard_map(shards, mesh=mesh, in_specs=in_specs, out_specs=out_specs, check_vma=False)
```
